256 devices in a mesh: dp: 32 (over z, x), cent: 8 (over y, core).
Axes of the slice: x: 4, y: 4, z: 8, core: 2. Of those that a mesh axis runs over, the one named last changes fastest.
Arguments:
- token_embeds: bfloat16 [32768, 128], P(('dp', 'cent')), may hold values from -60 to 60
- centroids: bfloat16 [65536, 128], P('cent'), may hold values from -20 to 20
- targets: int32 [32768], P(('dp', 'cent')), may hold values from 0 to 65535
- token_weights: bfloat16 [32768], P(('dp', 'cent')), may hold values from 1 to 8
Outputs:
- grad_tokens: float32 [32768, 128], P(('dp', 'cent'))
- grad_centroids: float32 [65536, 128], P('cent')
The draws below stay inside these ranges and needn't reach their ends.
All inputs are finite; a program needn't handle non-finite values.
Results may differ from the reference program's by a relative error of at most 0.00058.
Values may be sent and summed in bfloat16 or wider, within the bound.
No kernel may reach another device: no remote copies, remote signals or barrier semaphores. Data moves between devices by JAX's collectives and lax.ppermute only.
A program may use at most 64 MiB of HBM per device.

```python
import math
import jax
import jax.numpy as jnp
from jax import lax

D = 128
CENTROIDS = 65536
TOKENS = 32768


def base_entries(key, rows):
    normals = jnp.clip(jax.random.normal(key, (rows, D), jnp.float32), -4.0, 4.0)
    return normals


def draw_token_embeds(key, part):
    key = jax.random.fold_in(key, 1)
    key_rows, key_scales = jax.random.split(key, 2)
    scales = jnp.exp(jax.random.uniform(key_scales, (TOKENS, 1), jnp.float32, math.log(0.6), math.log(1.2)))
    result = base_entries(key_rows, TOKENS) * scales
    return result.astype(jnp.bfloat16)


def draw_centroids(key, part):
    key = jax.random.fold_in(key, 2)
    key_rows, key_scales = jax.random.split(key, 2)
    scales = jnp.exp(jax.random.uniform(key_scales, (CENTROIDS, 1), jnp.float32, math.log(0.9), math.log(1.1)))
    rising = 0.9 + 0.2 * jnp.arange(CENTROIDS, dtype=jnp.float32) / CENTROIDS
    result = base_entries(key_rows, CENTROIDS) * scales * rising[:, None]
    return result.astype(jnp.bfloat16)


def touch_ends(values, stream_key, least, largest):
    dims = values.shape
    spot = [jax.random.randint(jax.random.fold_in(stream_key, axis), (), 0, dims[axis]) for axis in range(len(dims))]
    values = values.at[tuple(spot)].set(least)
    longest = dims.index(max(dims))
    spot[longest] = (spot[longest] + 1) % dims[longest]
    return values.at[tuple(spot)].set(largest)


def steps_of(key, shape, shards, smallest, high):
    gain, own = 1.0, jax.random.fold_in(key, 6)
    for position, parts in shards:
        draws = jnp.exp(jax.random.uniform(jax.random.fold_in(own, position), (parts,), jnp.float32, smallest / len(shards), high / len(shards)))
        gain = gain * jnp.repeat(draws, shape[position] // parts).reshape([-1 if axis == position else 1 for axis in range(len(shape))])
    return gain


def setup_inputs(seed: int = 0) -> dict:
    streams_of = jax.random.split(jax.random.key(seed), 5)
    return {
        "token_embeds": draw_token_embeds(jax.random.fold_in(streams_of[4], 71), 0),
        "centroids": draw_centroids(jax.random.fold_in(streams_of[4], 71), 0),
        "targets": touch_ends(jax.random.randint(streams_of[2], (TOKENS,), 0, CENTROIDS), jax.random.fold_in(streams_of[2], 1), 0, CENTROIDS - 1).astype(jnp.int32),
        "token_weights": jnp.clip(jnp.exp(math.log(8.0) - 2.0794415 * jax.random.uniform(streams_of[3], (TOKENS,), jnp.float32) ** steps_of(streams_of[3], (TOKENS,), ((0, 256),), -0.2, 0.2)), 1.0, 8.0).astype(jnp.bfloat16),
    }


def reference(token_embeds, centroids, targets, token_weights):
    factor = 1.0 / math.sqrt(D)
    row_block = math.gcd(TOKENS, 1024)
    row_count = TOKENS // row_block
    embeds_split = token_embeds.reshape(row_count, row_block, D)
    targets_split = targets.reshape(row_count, row_block)
    weights_split = token_weights.reshape(row_count, row_block)
    centroid_ids = jnp.arange(CENTROIDS, dtype=jnp.int32)

    def accumulate(grad_total, pieces):
        embed_rows, target_rows, weight_rows = pieces
        logits = jnp.dot(embed_rows, centroids.T, preferred_element_type=jnp.float32) * factor
        row_peak = lax.optimization_barrier(jnp.max(logits, axis=1, keepdims=True))
        exponent = jnp.exp(logits - row_peak)
        row_sum = lax.optimization_barrier(jnp.sum(exponent, axis=1, keepdims=True))
        assignment = exponent / row_sum
        onehot = (target_rows[:, None] == centroid_ids[None, :]).astype(jnp.float32)
        slopes = (weight_rows.astype(jnp.float32)[:, None] * (assignment - onehot)).astype(jnp.bfloat16)
        token_part = jnp.dot(slopes, centroids, preferred_element_type=jnp.float32) * factor
        grad_total = grad_total + jnp.dot(slopes.T, embed_rows, preferred_element_type=jnp.float32)
        return (grad_total, token_part)
    grad_total, token_grads = lax.scan(accumulate, jnp.zeros((CENTROIDS, D), jnp.float32), (embeds_split, targets_split, weights_split))
    return (token_grads.reshape(TOKENS, D), grad_total * factor)
```

```python
import math

import jax
import jax.numpy as jnp
from jax import lax
from jax.sharding import PartitionSpec as P
from jax.experimental import pallas as pl
from jax.experimental.pallas import tpu as pltpu
A2 = math.log2(math.e) / math.sqrt(128.0)
F32=jnp.float32; BF=jnp.bfloat16
NT=(((1,),(1,)),((),()))

def p1_kernel(cc, g_ref, c_ref, out_ref, e_s, la, lb):
    for j in range(8):
        e_s[j*128:(j+1)*128,:] = g_ref[j,:128,:]
    e=e_s[...]
    n=c_ref.shape[0]//cc
    T=1024
    def dot(i, dst):
        c=c_ref[pl.ds(pl.multiple_of(i*cc,cc),cc),:]
        dst[...]=lax.dot_general(c,e,NT,preferred_element_type=F32)
    def proc(src,m,s):
        l=src[...].reshape(cc//8,8,T)
        mn=jnp.maximum(m,jnp.max(l,axis=0))
        p=jnp.exp2((l-mn[None])*A2)
        s=s*jnp.exp2((m-mn)*A2)+jnp.sum(p,axis=0)
        return mn,s
    dot(0,la)
    def body(k,ms):
        m,s=ms
        dot(2*k+1,lb)
        m,s=proc(la,m,s)
        dot(jnp.minimum(2*k+2,n-1),la)
        m,s=proc(lb,m,s)
        return m,s
    m0=jnp.full((8,T),-3.0e38,F32); s0=jnp.zeros((8,T),F32)
    m,s=lax.fori_loop(0,n//2,body,(m0,s0))
    mt=jnp.max(m,axis=0,keepdims=True)
    st=jnp.sum(s*jnp.exp2((m-mt)*A2),axis=0,keepdims=True)
    for j in range(8):
        out_ref[j:j+1,:]=mt[:,j*128:(j+1)*128]
        out_ref[8+j:9+j,:]=st[:,j*128:(j+1)*128]

def p1(g,cen,cc=512):
    return pl.pallas_call(
        lambda *r: p1_kernel(cc,*r),
        out_shape=jax.ShapeDtypeStruct((16,128),F32),
        scratch_shapes=[pltpu.VMEM((1024,128),BF),pltpu.VMEM((cc,1024),F32),pltpu.VMEM((cc,1024),F32)],
        compiler_params=pltpu.CompilerParams(vmem_limit_bytes=56*2**20),
        cost_estimate=pl.CostEstimate(flops=2*1024*8192*128,bytes_accessed=3*2**20,transcendentals=1024*8192),
        name="pass_one")(g,cen)

def encode(x, half):
    mx=jnp.max(jnp.abs(x),axis=0,keepdims=True)
    k=jnp.ceil(jnp.log2(jnp.maximum(mx,1e-35))*32.0)
    q=jnp.round(x*(jnp.exp2(k*(-1.0/32.0))*32700.0)).astype(jnp.int32)
    code=(q[:half]&0xFFFF)|(q[half:]<<16)
    return code,k.astype(jnp.int32)

def decode(code,k):
    sc=jnp.exp2(k.astype(F32)*(1.0/32.0))*(1.0/32700.0)
    lo=((code<<16)>>16).astype(F32)*sc
    hi=(code>>16).astype(F32)*sc
    return lo,hi

def p2_kernel(cc,tb,base_ref,g_ref,st_ref,c_ref,gc_ref,gt_ref,e_s,ct_s,M,R,W,TG,gcs,gts,la,lb,sa,sb):
    T=4096; C=c_ref.shape[0]
    io=lax.broadcasted_iota(jnp.int32,(8,128),0)
    base=base_ref[1]
    for xx in range(4):
        ms=[st_ref[xx*8+i,0:8,:] for i in range(8)]
        mm=ms[0]
        for v in ms[1:]: mm=jnp.maximum(mm,v)
        ss=sum(st_ref[xx*8+i,8:16,:]*jnp.exp2((ms[i]-mm)*A2) for i in range(8))
        for j in range(8):
            b=xx*8+j; sl=slice(b*128,(b+1)*128)
            e_s[sl,:]=g_ref[xx,j,:128,:]
            info=g_ref[xx,j,128:144,:].astype(F32)
            w=info[0:1,:]
            tg=(info[1:2,:]*256.0+info[2:3,:]).astype(jnp.int32)
            M[:,sl]=jnp.broadcast_to(mm[j:j+1,:],(8,128))
            R[:,sl]=jnp.broadcast_to(w/ss[j:j+1,:],(8,128))
            W[:,sl]=jnp.broadcast_to(w,(8,128))
            TG[:,sl]=jnp.broadcast_to(tg,(8,128))-io-base
    ct_s[...]=c_ref[...].T
    gts[...]=jnp.zeros_like(gts)
    nt=T//tb; n=(C//cc)*nt
    def ix(i):
        return pl.multiple_of((i//nt)*cc,cc), pl.multiple_of((i%nt)*tb,tb)
    def dot(i,dst):
        ci,ti=ix(i)
        dst[...]=lax.dot_general(c_ref[pl.ds(ci,cc),:],e_s[pl.ds(ti,tb),:],NT,preferred_element_type=F32)
    def proc(i,src,dst):
        ci,ti=ix(i); ts=pl.ds(ti,tb)
        l=src[...].reshape(cc//8,8,tb)
        p=jnp.exp2((l-M[:,ts][None])*A2)*R[:,ts][None]
        tgr=TG[:,ts]-ci
        k8=lax.broadcasted_iota(jnp.int32,(cc//8,8,tb),0)*8
        p=p-jnp.where(tgr[None]==k8,W[:,ts][None],0.0)
        dst[...]=p.reshape(cc,tb).astype(BF)
    def mm(i,src):
        ci,ti=ix(i)
        s=src[...]
        d=jnp.dot(s,e_s[pl.ds(ti,tb),:],preferred_element_type=F32)
        @pl.when(i%nt==0)
        def _(): gcs[pl.ds(ci,cc),:]=d
        @pl.when(i%nt!=0)
        def _(): gcs[pl.ds(ci,cc),:]+=d
        gts[:,pl.ds(ti,tb)]+=jnp.dot(ct_s[:,pl.ds(ci,cc)],s,preferred_element_type=F32)
    dot(0,la)
    def body(k,_):
        dot(2*k+1,lb)
        proc(2*k,la,sa)
        mm(2*k,sa)
        dot(jnp.minimum(2*k+2,n-1),la)
        proc(2*k+1,lb,sb)
        mm(2*k+1,sb)
        return 0
    lax.fori_loop(0,n//2,body,0)
    for z in range(8):
        code,k=encode(gcs[z*256:(z+1)*256,:],128)
        gc_ref[z,0:128,:]=code
        gc_ref[z,128:136,:]=jnp.broadcast_to(k,(8,128))
    for b in range(32):
        code,k=encode(gts[:,b*128:(b+1)*128],64)
        gt_ref[b,0:64,:]=code
        gt_ref[b,64:72,:]=jnp.broadcast_to(k,(8,128))

def p2(base,g,st,cen,cc=512,tb=1024):
    T=4096
    return pl.pallas_call(
        lambda *r: p2_kernel(cc,tb,*r),
        out_shape=(jax.ShapeDtypeStruct((8,136,128),jnp.int32),jax.ShapeDtypeStruct((32,72,128),jnp.int32)),
        grid_spec=pltpu.PrefetchScalarGridSpec(num_scalar_prefetch=1,grid=(1,),
            in_specs=[pl.BlockSpec((4,8,144,128),lambda i,b:(0,0,0,0)),
                      pl.BlockSpec((32,16,128),lambda i,b:(0,0,0)),
                      pl.BlockSpec((2048,128),lambda i,b:(b[0],0))],
            out_specs=[pl.BlockSpec((8,136,128),lambda i,b:(0,0,0)),pl.BlockSpec((32,72,128),lambda i,b:(0,0,0))],
            scratch_shapes=[pltpu.VMEM((T,128),BF),pltpu.VMEM((128,2048),BF),
                pltpu.VMEM((8,T),F32),pltpu.VMEM((8,T),F32),pltpu.VMEM((8,T),F32),pltpu.VMEM((8,T),jnp.int32),
                pltpu.VMEM((2048,128),F32),pltpu.VMEM((128,T),F32),
                pltpu.VMEM((cc,tb),F32),pltpu.VMEM((cc,tb),F32),pltpu.VMEM((cc,tb),BF),pltpu.VMEM((cc,tb),BF)]),
        compiler_params=pltpu.CompilerParams(vmem_limit_bytes=56*2**20),
        cost_estimate=pl.CostEstimate(flops=6*4096*2048*128,bytes_accessed=4*2**20,transcendentals=4096*2048),
        name="pass_two")(base,g,st,cen)


def sum_gc_kernel(in_ref, out_ref):
    lo = hi = None
    for z in range(8):
        a, b = decode(in_ref[z, 0:128, :], in_ref[z, 128:129, :])
        lo = a if lo is None else lo + a
        hi = b if hi is None else hi + b
    x = jnp.concatenate([lo, hi], axis=0) * (1.0 / math.sqrt(128.0))
    code, k = encode(x, 128)
    block = jnp.concatenate([code, jnp.broadcast_to(k, (8, 128))], axis=0)
    for z in range(8):
        out_ref[z] = block


def sum_gc(r):
    return pl.pallas_call(
        sum_gc_kernel,
        out_shape=jax.ShapeDtypeStruct((8, 136, 128), jnp.int32),
        cost_estimate=pl.CostEstimate(flops=2**21, bytes_accessed=2**20, transcendentals=0),
        name="sum_centroid_grads",
    )(r)


def narrow_kernel(in_ref, out_ref):
    for z in range(8):
        c = in_ref[z, 0:128, :]
        out_ref[z, 0:128, :] = ((c << 16) >> 16).astype(jnp.int16)
        out_ref[z, 128:256, :] = (c >> 16).astype(jnp.int16)
        k = in_ref[z, 128:136, :]
        out_ref[z, 256:272, :] = jnp.concatenate([k, k], axis=0).astype(jnp.int16)


def narrow(r):
    return pl.pallas_call(
        narrow_kernel,
        out_shape=jax.ShapeDtypeStruct((8, 272, 128), jnp.int16),
        cost_estimate=pl.CostEstimate(flops=2**20, bytes_accessed=2**20, transcendentals=0),
        name="narrow_codes",
    )(r)


def widen_kernel(in_ref, out_ref):
    for z in range(in_ref.shape[0]):
        k = in_ref[z, 256:272, :].astype(F32)[0:1]
        sc = jnp.exp2(k * (1.0 / 32.0)) * (1.0 / 32700.0)
        out_ref[z] = in_ref[z, 0:256, :].astype(F32) * sc


def widen(r, step=4):
    return pl.pallas_call(
        widen_kernel,
        grid=(32 // step,),
        in_specs=[pl.BlockSpec((step, 272, 128), lambda i: (i, 0, 0))],
        out_specs=pl.BlockSpec((step, 256, 128), lambda i: (i, 0, 0)),
        out_shape=jax.ShapeDtypeStruct((32, 256, 128), F32),
        cost_estimate=pl.CostEstimate(flops=2**22, bytes_accessed=6 * 2**20, transcendentals=0),
        name="widen_centroid_grads",
    )(r)


def sum_gt_kernel(in_ref, out_ref):
    lo = hi = None
    for b in range(32):
        a, h = decode(in_ref[b, 0:64, :], in_ref[b, 64:65, :])
        lo = a if lo is None else lo + a
        hi = h if hi is None else hi + h
    x = jnp.concatenate([lo, hi], axis=0) * (1.0 / math.sqrt(128.0))
    out_ref[...] = x.T


def sum_gt(r):
    return pl.pallas_call(
        sum_gt_kernel,
        out_shape=jax.ShapeDtypeStruct((128, 128), F32),
        cost_estimate=pl.CostEstimate(flops=2**20, bytes_accessed=2**20, transcendentals=0),
        name="sum_token_grads",
    )(r)


def spread(x, axes, n):
    return lax.all_to_all(jnp.broadcast_to(x[None], (n,) + x.shape), axes, 0, 0, tiled=True)


def local(token_embeds, centroids, targets, token_weights):
    info = jnp.stack([
        token_weights,
        (targets >> 8).astype(BF),
        (targets & 255).astype(BF),
    ])
    packed = jnp.concatenate([token_embeds, info, jnp.zeros((13, 128), BF)], axis=0)
    group = spread(packed, ("y", "c"), 8)
    plane = spread(group, "x", 4)
    stats = p1(group, centroids)
    all_stats = spread(stats, ("x", "y", "c"), 32)
    x = lax.axis_index("x")
    cent = lax.axis_index("y") * 2 + lax.axis_index("c")
    place = jnp.stack([x, cent * 8192 + x * 2048]).astype(jnp.int32)
    gc_codes, gt_codes = p2(place, plane, all_stats, centroids)
    gc_parts = lax.all_to_all(gc_codes, "z", 0, 0, tiled=True)
    gt_parts = lax.all_to_all(gt_codes, ("x", "y", "c"), 0, 0, tiled=True)
    gc_rows = sum_gc(gc_parts)
    gc_plane = lax.all_to_all(gc_rows, "z", 0, 0, tiled=True)
    gc_all = lax.all_gather(narrow(gc_plane), "x", axis=0, tiled=True)
    grad_centroids = widen(gc_all).reshape(8192, 128)
    grad_tokens = sum_gt(gt_parts)
    return grad_tokens, grad_centroids


def solution(mesh):
    torus = jax.sharding.Mesh(mesh.devices.reshape(8, 4, 4, 2), ("z", "x", "y", "c"))
    return jax.shard_map(
        local,
        mesh=torus,
        in_specs=(P(("z", "x", "y", "c"), None), P(("y", "c"), None), P(("z", "x", "y", "c")), P(("z", "x", "y", "c"))),
        out_specs=(P(("z", "x", "y", "c"), None), P(("y", "c"), None)),
        check_vma=False,
    )
```

```python
import math

import jax
import jax.numpy as jnp
from jax import lax
from jax.experimental import pallas as pl
from jax.experimental.pallas import tpu as pltpu
from jax.sharding import PartitionSpec as P

SCALE = 1.0 / math.sqrt(128.0)
RATE = math.log2(math.e) / math.sqrt(128.0)
F32 = jnp.float32
BF16 = jnp.bfloat16
TOP = 32700.0
STEPS = 32.0
VM = pl.BlockSpec(memory_space=pltpu.VMEM)


def dot(a, b, ca, cb):
    return lax.dot_general(a, b, (((ca,), (cb,)), ((), ())), preferred_element_type=F32)


def params(mib):
    return pltpu.CompilerParams(vmem_limit_bytes=mib * 2**20)


def cost(flops, transcendentals=0):
    return pl.CostEstimate(flops=flops, bytes_accessed=2**21, transcendentals=transcendentals)


def encode(x):
    largest = jnp.max(jnp.abs(x), axis=0, keepdims=True)
    k = jnp.ceil(jnp.log2(jnp.maximum(largest, 1e-35)) * STEPS)
    q = jnp.round(x * (jnp.exp2(k * (-1.0 / STEPS)) * TOP))
    return q.astype(jnp.int32).astype(jnp.int16), k.astype(jnp.int32).astype(jnp.int16)


def scale_of(k):
    return jnp.exp2(k.astype(F32) * (1.0 / STEPS)) * (1.0 / TOP)


def pass_one_kernel(rows, e_ref, c_ref, info_ref, out_ref, la, lb):
    T = 1024
    n = c_ref.shape[0] // rows

    def fill(i, dst, m):
        c = c_ref[pl.ds(pl.multiple_of(i * rows, rows), rows), :]
        l = dot(c, e_ref[...], 1, 1)
        dst[...] = l
        return jnp.maximum(m, jnp.max(l.reshape(rows // 8, 8, T), axis=0))

    def add(src, s, m_of_s, m):
        l = src[...].reshape(rows // 8, 8, T)
        return s * jnp.exp2((m_of_s - m) * RATE) + jnp.sum(jnp.exp2((l - m[None]) * RATE), axis=0)

    m_old = jnp.full((8, T), -3.0e38, F32)
    s = jnp.zeros((8, T), F32)
    m = fill(0, la, m_old)

    def body(k, state):
        m_old, m, s = state
        m_b = fill(2 * k + 1, lb, m)
        s = add(la, s, m_old, m)
        m_a = fill(jnp.minimum(2 * k + 2, n - 1), la, m_b)
        s = add(lb, s, m, m_b)
        return m_b, m_a, s

    m_old, m, s = lax.fori_loop(0, n // 2 - 1, body, (m_old, m, s))
    m_b = fill(n - 1, lb, m)
    s = add(la, s, m_old, m)
    s = add(lb, s, m, m_b)
    m = m_b
    peak = jnp.max(m, axis=0, keepdims=True)
    total = jnp.sum(s * jnp.exp2((m - peak) * RATE), axis=0, keepdims=True)
    for i in range(8):
        for j in range(8):
            out_ref[i, j : j + 1, :] = peak[:, j * 128 : (j + 1) * 128]
            out_ref[i, 8 + j : 9 + j, :] = total[:, j * 128 : (j + 1) * 128]
        out_ref[i, 16:24, :] = info_ref[...]


def pass_one(e, c, info, rows=1024):
    return pl.pallas_call(
        lambda *r: pass_one_kernel(rows, *r),
        in_specs=[VM] * 3,
        out_specs=VM,
        out_shape=jax.ShapeDtypeStruct((8, 24, 128), F32),
        scratch_shapes=[pltpu.VMEM((rows, 1024), F32)] * 2,
        compiler_params=params(24),
        cost_estimate=cost(8 * 2**30, 2**23),
        name="pass_one",
    )(e, c, info)


def combine_kernel(x_ref, out_ref):
    ms = [x_ref[i, 0:8, :] for i in range(8)]
    m = ms[0]
    for v in ms[1:]:
        m = jnp.maximum(m, v)
    s = sum(x_ref[i, 8:16, :] * jnp.exp2((ms[i] - m) * RATE) for i in range(8))
    for j in range(8):
        w = x_ref[j, 16:17, :]
        out_ref[j, 0:1, :] = m[j : j + 1]
        out_ref[j, 1:2, :] = w / s[j : j + 1]
        out_ref[j, 2:8, :] = x_ref[j, 16:22, :]


def combine(x):
    return pl.pallas_call(
        combine_kernel,
        in_specs=[VM],
        out_specs=VM,
        out_shape=jax.ShapeDtypeStruct((8, 8, 128), F32),
        cost_estimate=cost(2**16),
        name="combine",
    )(x)


def token_kernel(rows, base_ref, e_ref, st_ref, c_ref, out_ref, M, R, W, G, acc, la, lb, sa, sb):
    T = 1024
    n = c_ref.shape[0] // rows
    sub = lax.broadcasted_iota(jnp.int32, (8, 128), 0)
    for j in range(8):
        sl = slice(j * 128, (j + 1) * 128)
        M[:, sl] = jnp.broadcast_to(st_ref[j, 0:1, :], (8, 128))
        R[:, sl] = jnp.broadcast_to(st_ref[j, 1:2, :], (8, 128))
        W[:, sl] = jnp.broadcast_to(st_ref[j, 2:3, :], (8, 128))
        G[:, sl] = jnp.broadcast_to(st_ref[j, 3:4, :], (8, 128)).astype(jnp.int32) - sub - base_ref[0]
    acc[...] = jnp.zeros_like(acc)

    def at(i):
        return pl.ds(pl.multiple_of(i * rows, rows), rows)

    def fill(i, dst):
        dst[...] = dot(c_ref[at(i), :], e_ref[...], 1, 1)

    def slope(i, src, dst):
        l = src[...].reshape(rows // 8, 8, T)
        p = jnp.exp2((l - M[...][None]) * RATE) * R[...][None]
        k8 = lax.broadcasted_iota(jnp.int32, (rows // 8, 8, T), 0) * 8
        p = p - jnp.where((G[...] - i * rows)[None] == k8, W[...][None], 0.0)
        dst[...] = p.reshape(rows, T).astype(BF16)

    def add(i, src):
        acc[...] += dot(c_ref[at(i), :], src[...], 0, 0)

    fill(0, la)
    fill(1, lb)
    slope(0, la, sa)

    def body(k, _):
        fill(2 * k + 2, la)
        slope(2 * k + 1, lb, sb)
        add(2 * k, sa)
        fill(2 * k + 3, lb)
        slope(2 * k + 2, la, sa)
        add(2 * k + 1, sb)
        return 0

    lax.fori_loop(0, n // 2 - 1, body, 0)
    slope(n - 1, lb, sb)
    add(n - 2, sa)
    add(n - 1, sb)
    out_ref[...] = acc[...].T * SCALE


def token_grads(base, e, st, c, rows=1024):
    return pl.pallas_call(
        lambda *r: token_kernel(rows, *r),
        in_specs=[pl.BlockSpec(memory_space=pltpu.SMEM)] + [VM] * 3,
        out_specs=VM,
        out_shape=jax.ShapeDtypeStruct((1024, 128), F32),
        scratch_shapes=[pltpu.VMEM((8, 1024), F32)] * 3
        + [pltpu.VMEM((8, 1024), jnp.int32), pltpu.VMEM((128, 1024), F32)]
        + [pltpu.VMEM((rows, 1024), F32)] * 2
        + [pltpu.VMEM((rows, 1024), BF16)] * 2,
        compiler_params=params(32),
        cost_estimate=cost(12 * 2**30, 2**23),
        name="token_grads",
    )(base, e, st, c)


def centroid_kernel(T, base_ref, e0, e1, e2, e3, s0, s1, s2, s3, c_ref, out_ref, E, ET, ST, acc, la, lb, sa, sb):
    N = 2048
    n = 4096 // T
    c = c_ref[pl.ds(pl.multiple_of(base_ref[1], N), N), :]
    for x, (e, s) in enumerate(((e0, s0), (e1, s1), (e2, s2), (e3, s3))):
        E[x * 1024 : (x + 1) * 1024, :] = e[...]
        for j in range(8):
            b = x * 8 + j
            ST[b * 128 : (b + 1) * 128, :] = s[j].T
        ET[:, x * 1024 : (x + 1) * 1024] = e[...].T
    acc[...] = jnp.zeros_like(acc)
    base = base_ref[0] + base_ref[1]

    def at(i):
        return pl.ds(pl.multiple_of(i * T, T), T)

    def fill(i, dst):
        dst[...] = dot(E[at(i), :], c, 1, 1)

    def slope(i, src, dst):
        st = ST[at(i), :]
        p = jnp.exp2((src[...] - st[:, 0:1]) * RATE) * st[:, 1:2]
        place = lax.broadcasted_iota(jnp.int32, (T, N), 1)
        hit = (st[:, 3:4].astype(jnp.int32) - base) == place
        dst[...] = (p - jnp.where(hit, st[:, 2:3], 0.0)).astype(BF16)

    def add(i, src):
        acc[...] += dot(ET[:, at(i)], src[...], 1, 0)

    fill(0, la)
    fill(1, lb)
    slope(0, la, sa)

    def body(k, _):
        fill(2 * k + 2, la)
        slope(2 * k + 1, lb, sb)
        add(2 * k, sa)
        fill(2 * k + 3, lb)
        slope(2 * k + 2, la, sa)
        add(2 * k + 1, sb)
        return 0

    lax.fori_loop(0, n // 2 - 1, body, 0)
    slope(n - 1, lb, sb)
    add(n - 2, sa)
    add(n - 1, sb)
    for z in range(8):
        q, k = encode(acc[:, z * 256 : (z + 1) * 256])
        out_ref[z, 0:128, :] = q
        out_ref[z, 128:144, :] = jnp.broadcast_to(k, (16, 256))


def centroid_grads(base, es, sts, c, T=512):
    return pl.pallas_call(
        lambda *r: centroid_kernel(T, *r),
        in_specs=[pl.BlockSpec(memory_space=pltpu.SMEM)] + [VM] * 9,
        out_specs=VM,
        out_shape=jax.ShapeDtypeStruct((8, 144, 256), jnp.int16),
        scratch_shapes=[
            pltpu.VMEM((4096, 128), BF16),
            pltpu.VMEM((128, 4096), BF16),
            pltpu.VMEM((4096, 8), F32),
            pltpu.VMEM((128, 2048), F32),
            pltpu.VMEM((T, 2048), F32),
            pltpu.VMEM((T, 2048), F32),
            pltpu.VMEM((T, 2048), BF16),
            pltpu.VMEM((T, 2048), BF16),
        ],
        compiler_params=params(32),
        cost_estimate=cost(12 * 2**30, 2**23),
        name="centroid_grads",
    )(base, *es, *sts, c)


def sum_kernel(in_ref, out_ref):
    total = None
    for z in range(8):
        part = in_ref[z, 0:128, :].astype(F32) * scale_of(in_ref[z, 128:144, :])[0:1]
        total = part if total is None else total + part
    q, k = encode(total.T * SCALE)
    block = jnp.concatenate([q, jnp.broadcast_to(k, (16, 128))], axis=0)
    for z in range(8):
        out_ref[z] = block


def sum_planes(r):
    return pl.pallas_call(
        sum_kernel,
        in_specs=[VM],
        out_specs=VM,
        out_shape=jax.ShapeDtypeStruct((8, 272, 128), jnp.int16),
        cost_estimate=cost(2**22),
        name="sum_planes",
    )(r)


def widen(r):
    return r[:, 0:256, :].astype(F32) * scale_of(r[:, 256:257, :])


def shift(x, k):
    return lax.ppermute(x, "x", [(i, (i + k) % 4) for i in range(4)])


def ring(x):
    return [x, shift(x, 1), shift(x, 3), shift(x, 2)]


def local(token_embeds, centroids, targets, token_weights):
    info = jnp.stack([token_weights.astype(F32), targets.astype(F32)])
    info = jnp.concatenate([info, jnp.zeros((6, 128), F32)], axis=0)
    spread = jnp.broadcast_to(token_embeds[None], (8, 128, 128))
    group = lax.all_to_all(spread, ("y", "c"), 0, 0, tiled=True).reshape(1024, 128)
    plane = ring(group)
    stats = lax.all_to_all(pass_one(group, centroids, info), ("y", "c"), 0, 0, tiled=True)
    stats = combine(stats)
    plane_stats = ring(stats)
    cent = lax.axis_index("y") * 2 + lax.axis_index("c")
    base = jnp.stack([cent * 8192, lax.axis_index("x") * 2048]).astype(jnp.int32)
    token_part = token_grads(base, group, stats, centroids)
    grad_tokens = lax.psum_scatter(token_part, ("y", "c"), scatter_dimension=0, tiled=True)
    codes = centroid_grads(base, plane, plane_stats, centroids)
    codes = sum_planes(lax.all_to_all(codes, "z", 0, 0, tiled=True))
    codes = lax.all_to_all(codes, "z", 0, 0, tiled=True)
    codes = lax.all_gather(codes, "x", axis=0, tiled=True)
    return grad_tokens, widen(codes).reshape(8192, 128)


def solution(mesh):
    torus = jax.sharding.Mesh(mesh.devices.reshape(8, 4, 4, 2), ("z", "x", "y", "c"))
    tokens = P(("z", "x", "y", "c"))
    return jax.shard_map(
        local,
        mesh=torus,
        in_specs=(P(("z", "x", "y", "c"), None), P(("y", "c"), None), tokens, tokens),
        out_specs=(P(("z", "x", "y", "c"), None), P(("y", "c"), None)),
        check_vma=False,
    )
```

```python
import math

import jax
import jax.numpy as jnp
from jax import lax
from jax.experimental import pallas as pl
from jax.experimental.pallas import tpu as pltpu
from jax.sharding import PartitionSpec as P

SCALE = 1.0 / math.sqrt(128.0)
RATE = math.log2(math.e) / math.sqrt(128.0)
F32 = jnp.float32
BF16 = jnp.bfloat16
TOP = 32700.0
STEPS = 32.0
VM = pl.BlockSpec(memory_space=pltpu.VMEM)


def dot(a, b, ca, cb):
    return lax.dot_general(a, b, (((ca,), (cb,)), ((), ())), preferred_element_type=F32)


def params(mib):
    return pltpu.CompilerParams(vmem_limit_bytes=mib * 2**20)


def cost(flops, transcendentals=0):
    return pl.CostEstimate(flops=flops, bytes_accessed=2**21, transcendentals=transcendentals)


def encode(x):
    largest = jnp.max(jnp.abs(x), axis=0, keepdims=True)
    k = jnp.ceil(jnp.log2(jnp.maximum(largest, 1e-35)) * STEPS)
    q = jnp.round(x * (jnp.exp2(k * (-1.0 / STEPS)) * TOP))
    return q.astype(jnp.int32).astype(jnp.int16), k.astype(jnp.int32).astype(jnp.int16)


def scale_of(k):
    return jnp.exp2(k.astype(F32) * (1.0 / STEPS)) * (1.0 / TOP)


def pass_one_kernel(rows, e_ref, c_ref, info_ref, out_ref, la, lb):
    T = 1024
    n = c_ref.shape[0] // rows

    def fill(i, dst, m):
        c = c_ref[pl.ds(pl.multiple_of(i * rows, rows), rows), :]
        l = dot(c, e_ref[...], 1, 1)
        dst[...] = l
        return jnp.maximum(m, jnp.max(l.reshape(rows // 8, 8, T), axis=0))

    def add(src, s, m_of_s, m):
        l = src[...].reshape(rows // 8, 8, T)
        return s * jnp.exp2((m_of_s - m) * RATE) + jnp.sum(jnp.exp2((l - m[None]) * RATE), axis=0)

    m_old = jnp.full((8, T), -3.0e38, F32)
    s = jnp.zeros((8, T), F32)
    m = fill(0, la, m_old)

    def body(k, state):
        m_old, m, s = state
        m_b = fill(2 * k + 1, lb, m)
        s = add(la, s, m_old, m)
        m_a = fill(jnp.minimum(2 * k + 2, n - 1), la, m_b)
        s = add(lb, s, m, m_b)
        return m_b, m_a, s

    m_old, m, s = lax.fori_loop(0, n // 2 - 1, body, (m_old, m, s))
    m_b = fill(n - 1, lb, m)
    s = add(la, s, m_old, m)
    s = add(lb, s, m, m_b)
    m = m_b
    peak = jnp.max(m, axis=0, keepdims=True)
    total = jnp.sum(s * jnp.exp2((m - peak) * RATE), axis=0, keepdims=True)
    cut = [slice(j * 128, (j + 1) * 128) for j in range(8)]
    peaks = jnp.concatenate([peak[:, c] for c in cut], axis=0)
    totals = jnp.concatenate([total[:, c] for c in cut], axis=0)
    for i in range(32):
        out_ref[i, 0:8, :] = peaks
        out_ref[i, 8:16, :] = totals
        out_ref[i, 16:24, :] = info_ref[...]


def pass_one(e, c, info, rows=1024):
    return pl.pallas_call(
        lambda *r: pass_one_kernel(rows, *r),
        in_specs=[VM] * 3,
        out_specs=VM,
        out_shape=jax.ShapeDtypeStruct((32, 24, 128), F32),
        scratch_shapes=[pltpu.VMEM((rows, 1024), F32)] * 2,
        compiler_params=params(24),
        cost_estimate=cost(8 * 2**30, 2**23),
        name="pass_one",
    )(e, c, info)


def combine(x_ref, x):
    parts = [x_ref[x * 8 + i] for i in range(8)]
    m = parts[0][0:8]
    for v in parts[1:]:
        m = jnp.maximum(m, v[0:8])
    s = sum(v[8:16] * jnp.exp2((v[0:8] - m) * RATE) for v in parts)
    w = jnp.concatenate([v[16:17] for v in parts], axis=0)
    g = jnp.concatenate([v[17:18] for v in parts], axis=0)
    return m, w / s, w, g


def token_kernel(rows, base_ref, e_ref, st_ref, c_ref, out_ref, M, R, W, G, acc, la, lb, sa, sb):
    T = 1024
    n = c_ref.shape[0] // rows
    sub = lax.broadcasted_iota(jnp.int32, (8, 128), 0)
    m, r, w, g = combine(st_ref, base_ref[2])
    for j in range(8):
        sl = slice(j * 128, (j + 1) * 128)
        M[:, sl] = jnp.broadcast_to(m[j : j + 1], (8, 128))
        R[:, sl] = jnp.broadcast_to(r[j : j + 1], (8, 128))
        W[:, sl] = jnp.broadcast_to(w[j : j + 1], (8, 128))
        G[:, sl] = jnp.broadcast_to(g[j : j + 1], (8, 128)).astype(jnp.int32) - sub - base_ref[0]
    acc[...] = jnp.zeros_like(acc)

    def at(i):
        return pl.ds(pl.multiple_of(i * rows, rows), rows)

    def fill(i, dst):
        dst[...] = dot(c_ref[at(i), :], e_ref[...], 1, 1)

    def slope(i, src, dst):
        l = src[...].reshape(rows // 8, 8, T)
        p = jnp.exp2((l - M[...][None]) * RATE) * R[...][None]
        k8 = lax.broadcasted_iota(jnp.int32, (rows // 8, 8, T), 0) * 8
        p = p - jnp.where((G[...] - i * rows)[None] == k8, W[...][None], 0.0)
        dst[...] = p.reshape(rows, T).astype(BF16)

    def add(i, src):
        acc[...] += dot(c_ref[at(i), :], src[...], 0, 0)

    fill(0, la)
    fill(1, lb)
    slope(0, la, sa)

    def body(k, _):
        fill(2 * k + 2, la)
        slope(2 * k + 1, lb, sb)
        add(2 * k, sa)
        fill(2 * k + 3, lb)
        slope(2 * k + 2, la, sa)
        add(2 * k + 1, sb)
        return 0

    lax.fori_loop(0, n // 2 - 1, body, 0)
    slope(n - 1, lb, sb)
    add(n - 2, sa)
    add(n - 1, sb)
    for j in range(8):
        q, k = encode(acc[:, j * 128 : (j + 1) * 128])
        out_ref[j, 0:128, :] = q
        out_ref[j, 128:144, :] = jnp.broadcast_to(k, (16, 128))


def token_grads(base, e, st, c, rows=2048):
    return pl.pallas_call(
        lambda *r: token_kernel(rows, *r),
        in_specs=[pl.BlockSpec(memory_space=pltpu.SMEM)] + [VM] * 3,
        out_specs=VM,
        out_shape=jax.ShapeDtypeStruct((8, 144, 128), jnp.int16),
        scratch_shapes=[pltpu.VMEM((8, 1024), F32)] * 3
        + [pltpu.VMEM((8, 1024), jnp.int32), pltpu.VMEM((128, 1024), F32)]
        + [pltpu.VMEM((rows, 1024), F32)] * 2
        + [pltpu.VMEM((rows, 1024), BF16)] * 2,
        compiler_params=params(40),
        cost_estimate=cost(12 * 2**30, 2**23),
        name="token_grads",
    )(base, e, st, c)


def centroid_kernel(T, base_ref, e0, e1, e2, e3, st_ref, c_ref, out_ref, E, ET, ST, acc, la, lb, sa, sb):
    N = 2048
    n = 4096 // T
    c = c_ref[pl.ds(pl.multiple_of(base_ref[1], N), N), :]
    for x, (e, step) in enumerate(((e0, 0), (e1, 3), (e2, 1), (e3, 2))):
        E[x * 1024 : (x + 1) * 1024, :] = e[...]
        stats = combine(st_ref, lax.rem(base_ref[2] + step, 4))
        for j in range(8):
            b = x * 8 + j
            tile = jnp.concatenate([v[j : j + 1] for v in stats] + [jnp.zeros((4, 128), F32)], axis=0)
            ST[b * 128 : (b + 1) * 128, :] = tile.T
        ET[:, x * 1024 : (x + 1) * 1024] = e[...].T
    acc[...] = jnp.zeros_like(acc)
    base = base_ref[0] + base_ref[1]

    def at(i):
        return pl.ds(pl.multiple_of(i * T, T), T)

    def fill(i, dst):
        dst[...] = dot(E[at(i), :], c, 1, 1)

    def slope(i, src, dst):
        st = ST[at(i), :]
        p = jnp.exp2((src[...] - st[:, 0:1]) * RATE) * st[:, 1:2]
        place = lax.broadcasted_iota(jnp.int32, (T, N), 1)
        hit = (st[:, 3:4].astype(jnp.int32) - base) == place
        dst[...] = (p - jnp.where(hit, st[:, 2:3], 0.0)).astype(BF16)

    def add(i, src):
        acc[...] += dot(ET[:, at(i)], src[...], 1, 0)

    fill(0, la)
    fill(1, lb)
    slope(0, la, sa)

    def body(k, _):
        fill(2 * k + 2, la)
        slope(2 * k + 1, lb, sb)
        add(2 * k, sa)
        fill(2 * k + 3, lb)
        slope(2 * k + 2, la, sa)
        add(2 * k + 1, sb)
        return 0

    lax.fori_loop(0, n // 2 - 1, body, 0)
    slope(n - 1, lb, sb)
    add(n - 2, sa)
    add(n - 1, sb)
    for z in range(8):
        q, k = encode(acc[:, z * 256 : (z + 1) * 256])
        out_ref[z, 0:128, :] = q
        out_ref[z, 128:144, :] = jnp.broadcast_to(k, (16, 256))


def centroid_grads(base, es, st, c, T=1024):
    return pl.pallas_call(
        lambda *r: centroid_kernel(T, *r),
        in_specs=[pl.BlockSpec(memory_space=pltpu.SMEM)] + [VM] * 6,
        out_specs=VM,
        out_shape=jax.ShapeDtypeStruct((8, 144, 256), jnp.int16),
        scratch_shapes=[
            pltpu.VMEM((4096, 128), BF16),
            pltpu.VMEM((128, 4096), BF16),
            pltpu.VMEM((4096, 8), F32),
            pltpu.VMEM((128, 2048), F32),
            pltpu.VMEM((T, 2048), F32),
            pltpu.VMEM((T, 2048), F32),
            pltpu.VMEM((T, 2048), BF16),
            pltpu.VMEM((T, 2048), BF16),
        ],
        compiler_params=params(48),
        cost_estimate=cost(12 * 2**30, 2**23),
        name="centroid_grads",
    )(base, *es, st, c)


def total_of(parts):
    total = None
    for ref in parts:
        part = ref[0:128, :].astype(F32) * scale_of(ref[128:144, :])[0:1]
        total = part if total is None else total + part
    return total.T * SCALE


def sum_tokens_kernel(*refs):
    refs[8][...] = total_of(refs[:8])


def sum_tokens(r):
    return pl.pallas_call(
        sum_tokens_kernel,
        in_specs=[VM] * 8,
        out_specs=VM,
        out_shape=jax.ShapeDtypeStruct((128, 128), F32),
        cost_estimate=cost(2**18),
        name="sum_tokens",
    )(*r)


def sum_kernel(in_ref, out_ref):
    q, k = encode(total_of([in_ref.at[z] for z in range(8)]))
    block = jnp.concatenate([q, jnp.broadcast_to(k, (16, 128))], axis=0)
    for z in range(8):
        out_ref[z] = block


def sum_planes(r):
    return pl.pallas_call(
        sum_kernel,
        in_specs=[VM],
        out_specs=VM,
        out_shape=jax.ShapeDtypeStruct((8, 272, 128), jnp.int16),
        cost_estimate=cost(2**22),
        name="sum_planes",
    )(r)


def widen(r):
    return r[:, 0:256, :].astype(F32) * scale_of(r[:, 256:257, :])


def shift(x, k):
    return lax.ppermute(x, "x", [(i, (i + k) % 4) for i in range(4)])


def ring(x):
    return [x, shift(x, 1), shift(x, 3), shift(x, 2)]


def exchange(x, me):
    out = [lax.dynamic_index_in_dim(x, me, 0, keepdims=False)]
    for k in range(1, 8):
        block = lax.dynamic_index_in_dim(x, me ^ k, 0, keepdims=False)
        out.append(lax.ppermute(block, ("y", "c"), [(i, i ^ k) for i in range(8)]))
    return out


def local(token_embeds, centroids, targets, token_weights):
    info = jnp.stack([token_weights.astype(F32), targets.astype(F32)])
    info = jnp.concatenate([info, jnp.zeros((6, 128), F32)], axis=0)
    spread = jnp.broadcast_to(token_embeds[None], (8, 128, 128))
    group = lax.all_to_all(spread, ("y", "c"), 0, 0, tiled=True).reshape(1024, 128)
    plane = ring(group)
    stats = pass_one(group, centroids, info)
    stats, *plane = lax.optimization_barrier((stats, *plane))
    stats = lax.all_to_all(stats, ("x", "y", "c"), 0, 0, tiled=True)
    cent = lax.axis_index("y") * 2 + lax.axis_index("c")
    x = lax.axis_index("x")
    base = jnp.stack([cent * 8192, x * 2048, x]).astype(jnp.int32)
    codes = centroid_grads(base, plane, stats, centroids)
    codes = lax.all_to_all(codes, "z", 0, 0, tiled=True)
    token_codes = token_grads(base, group, stats, centroids)
    codes = sum_planes(codes)
    codes, token_codes = lax.optimization_barrier((codes, token_codes))
    parts = exchange(token_codes, cent)
    codes = lax.all_to_all(codes, "z", 0, 0, tiled=True)
    codes = lax.all_gather(codes, "x", axis=0, tiled=True)
    return sum_tokens(parts), widen(codes).reshape(8192, 128)


def solution(mesh):
    torus = jax.sharding.Mesh(mesh.devices.reshape(8, 4, 4, 2), ("z", "x", "y", "c"))
    tokens = P(("z", "x", "y", "c"))
    return jax.shard_map(
        local,
        mesh=torus,
        in_specs=(P(("z", "x", "y", "c"), None), P(("y", "c"), None), tokens, tokens),
        out_specs=(P(("z", "x", "y", "c"), None), P(("y", "c"), None)),
        check_vma=False,
    )
```

```python
import math

import jax
import jax.numpy as jnp
from jax import lax
from jax.experimental import pallas as pl
from jax.experimental.pallas import tpu as pltpu
from jax.sharding import PartitionSpec as P

SCALE = 1.0 / math.sqrt(128.0)
RATE = math.log2(math.e) / math.sqrt(128.0)
F32 = jnp.float32
BF16 = jnp.bfloat16
TOP = 32700.0
STEPS = 32.0
VM = pl.BlockSpec(memory_space=pltpu.VMEM)
SM = pl.BlockSpec(memory_space=pltpu.SMEM)
RING = (0, 1, 3, 2)


def dot(a, b, ca, cb):
    return lax.dot_general(a, b, (((ca,), (cb,)), ((), ())), preferred_element_type=F32)


def params(mib):
    return pltpu.CompilerParams(vmem_limit_bytes=mib * 2**20)


def cost(flops, transcendentals=0):
    return pl.CostEstimate(flops=flops, bytes_accessed=2**21, transcendentals=transcendentals)


def encode(x):
    largest = jnp.max(jnp.abs(x), axis=0, keepdims=True)
    k = jnp.ceil(jnp.log2(jnp.maximum(largest, 1e-35)) * STEPS)
    q = jnp.round(x * (jnp.exp2(k * (-1.0 / STEPS)) * TOP))
    return q.astype(jnp.int32).astype(jnp.int16), k.astype(jnp.int32).astype(jnp.int16)


def scale_of(k):
    return jnp.exp2(k.astype(F32) * (1.0 / STEPS)) * (1.0 / TOP)


def owner(base_ref, k):
    y = lax.rem(base_ref[3] + 4 - RING[k // 2], 4)
    return y * 2 + lax.rem(base_ref[4] + k % 2, 2)


def arrange(base_ref, slots_ref, out_ref, first=0):
    for k in range(8):
        at = pl.multiple_of((first + owner(base_ref, k)) * 128, 128)
        out_ref[pl.ds(at, 128), :] = slots_ref[k * 128 : (k + 1) * 128, :]


def pass_one_kernel(rows, base_ref, e_ref, c_ref, info_ref, out_ref, order, la, lb):
    T = 1024
    n = c_ref.shape[0] // rows

    def fill(i, dst, m):
        c = c_ref[pl.ds(pl.multiple_of(i * rows, rows), rows), :]
        l = dot(c, e_ref[...], 1, 1)
        dst[...] = l
        return jnp.maximum(m, jnp.max(l.reshape(rows // 8, 8, T), axis=0))

    def add(src, s, m_of_s, m):
        l = src[...].reshape(rows // 8, 8, T)
        return s * jnp.exp2((m_of_s - m) * RATE) + jnp.sum(jnp.exp2((l - m[None]) * RATE), axis=0)

    m_old = jnp.full((8, T), -3.0e38, F32)
    s = jnp.zeros((8, T), F32)
    m = fill(0, la, m_old)

    def body(k, state):
        m_old, m, s = state
        m_b = fill(2 * k + 1, lb, m)
        s = add(la, s, m_old, m)
        m_a = fill(2 * k + 2, la, m_b)
        s = add(lb, s, m, m_b)
        return m_b, m_a, s

    m_old, m, s = lax.fori_loop(0, n // 2 - 1, body, (m_old, m, s))
    m_b = fill(n - 1, lb, m)
    s = add(la, s, m_old, m)
    s = add(lb, s, m, m_b)
    m = m_b
    peak = jnp.max(m, axis=0, keepdims=True)
    total = jnp.sum(s * jnp.exp2((m - peak) * RATE), axis=0, keepdims=True)
    for k in range(8):
        j = owner(base_ref, k)
        order[pl.ds(j, 1), :] = peak[:, k * 128 : (k + 1) * 128]
        order[pl.ds(8 + j, 1), :] = total[:, k * 128 : (k + 1) * 128]
    stats = order[...]
    for i in range(32):
        out_ref[i, 0:16, :] = stats
        out_ref[i, 16:24, :] = info_ref[...]


def pass_one(base, e, c, info, rows=1024):
    return pl.pallas_call(
        lambda *r: pass_one_kernel(rows, *r),
        in_specs=[SM, VM, VM, VM],
        out_specs=VM,
        out_shape=jax.ShapeDtypeStruct((32, 24, 128), F32),
        scratch_shapes=[
            pltpu.VMEM((16, 128), F32),
            pltpu.VMEM((rows, 1024), F32),
            pltpu.VMEM((rows, 1024), F32),
        ],
        compiler_params=params(24),
        cost_estimate=cost(8 * 2**30, 2**23),
        name="pass_one",
    )(base, e, c, info)


def combine(x_ref, x):
    parts = [x_ref[x * 8 + i] for i in range(8)]
    m = parts[0][0:8]
    for v in parts[1:]:
        m = jnp.maximum(m, v[0:8])
    s = sum(v[8:16] * jnp.exp2((v[0:8] - m) * RATE) for v in parts)
    w = jnp.concatenate([v[16:17] for v in parts], axis=0)
    g = jnp.concatenate([v[17:18] for v in parts], axis=0)
    return m, w / s, w, g


def token_kernel(rows, base_ref, slots_ref, st_ref, c_ref, out_ref, e_ref, M, R, W, G, acc, la, lb, sa, sb):
    T = 1024
    n = c_ref.shape[0] // rows
    sub = lax.broadcasted_iota(jnp.int32, (8, 128), 0)
    arrange(base_ref, slots_ref, e_ref)
    m, r, w, g = combine(st_ref, base_ref[2])
    for j in range(8):
        sl = slice(j * 128, (j + 1) * 128)
        M[:, sl] = jnp.broadcast_to(m[j : j + 1], (8, 128))
        R[:, sl] = jnp.broadcast_to(r[j : j + 1], (8, 128))
        W[:, sl] = jnp.broadcast_to(w[j : j + 1], (8, 128))
        G[:, sl] = jnp.broadcast_to(g[j : j + 1], (8, 128)).astype(jnp.int32) - sub - base_ref[0]
    acc[...] = jnp.zeros_like(acc)

    def at(i):
        return pl.ds(pl.multiple_of(i * rows, rows), rows)

    def fill(i, dst):
        dst[...] = dot(c_ref[at(i), :], e_ref[...], 1, 1)

    def slope(i, src, dst):
        l = src[...].reshape(rows // 8, 8, T)
        p = jnp.exp2((l - M[...][None]) * RATE) * R[...][None]
        k8 = lax.broadcasted_iota(jnp.int32, (rows // 8, 8, T), 0) * 8
        p = p - jnp.where((G[...] - i * rows)[None] == k8, W[...][None], 0.0)
        dst[...] = p.reshape(rows, T).astype(BF16)

    def add(i, src):
        acc[...] += dot(c_ref[at(i), :], src[...], 0, 0)

    fill(0, la)
    fill(1, lb)
    slope(0, la, sa)

    def body(k, _):
        fill(2 * k + 2, la)
        slope(2 * k + 1, lb, sb)
        add(2 * k, sa)
        fill(2 * k + 3, lb)
        slope(2 * k + 2, la, sa)
        add(2 * k + 1, sb)
        return 0

    lax.fori_loop(0, n // 2 - 1, body, 0)
    slope(n - 1, lb, sb)
    add(n - 2, sa)
    add(n - 1, sb)
    for j in range(8):
        q, k = encode(acc[:, j * 128 : (j + 1) * 128])
        out_ref[j, 0:128, :] = q
        out_ref[j, 128:144, :] = jnp.broadcast_to(k, (16, 128))


def token_grads(base, e, st, c, rows=2048):
    return pl.pallas_call(
        lambda *r: token_kernel(rows, *r),
        in_specs=[SM, VM, VM, VM],
        out_specs=VM,
        out_shape=jax.ShapeDtypeStruct((8, 144, 128), jnp.int16),
        scratch_shapes=[
            pltpu.VMEM((1024, 128), BF16),
        ]
        + [pltpu.VMEM((8, 1024), F32)] * 3
        + [pltpu.VMEM((8, 1024), jnp.int32), pltpu.VMEM((128, 1024), F32)]
        + [pltpu.VMEM((rows, 1024), F32)] * 2
        + [pltpu.VMEM((rows, 1024), BF16)] * 2,
        compiler_params=params(40),
        cost_estimate=cost(12 * 2**30, 2**23),
        name="token_grads",
    )(base, e, st, c)


def centroid_kernel(T, base_ref, e0, e1, e2, e3, st_ref, c_ref, out_ref, E, ET, ST, acc, la, lb, sa, sb):
    N = 2048
    n = 4096 // T
    c = c_ref[pl.ds(pl.multiple_of(base_ref[1], N), N), :]
    arrange(base_ref, e0, E)
    la[...] = dot(E[0:T, :], c, 1, 1)
    for x, e in enumerate((e1, e2, e3)):
        arrange(base_ref, e, E, 8 + x * 8)
    for x, step in enumerate((0, 3, 1, 2)):
        stats = combine(st_ref, lax.rem(base_ref[2] + step, 4))
        for j in range(8):
            b = x * 8 + j
            tile = jnp.concatenate([v[j : j + 1] for v in stats] + [jnp.zeros((4, 128), F32)], axis=0)
            ST[b * 128 : (b + 1) * 128, :] = tile.T
        ET[:, x * 1024 : (x + 1) * 1024] = E[x * 1024 : (x + 1) * 1024, :].T
    acc[...] = jnp.zeros_like(acc)
    base = base_ref[0] + base_ref[1]

    def at(i):
        return pl.ds(pl.multiple_of(i * T, T), T)

    def fill(i, dst):
        dst[...] = dot(E[at(i), :], c, 1, 1)

    def slope(i, src, dst):
        st = ST[at(i), :]
        p = jnp.exp2((src[...] - st[:, 0:1]) * RATE) * st[:, 1:2]
        place = lax.broadcasted_iota(jnp.int32, (T, N), 1)
        hit = (st[:, 3:4].astype(jnp.int32) - base) == place
        dst[...] = (p - jnp.where(hit, st[:, 2:3], 0.0)).astype(BF16)

    def add(i, src):
        acc[...] += dot(ET[:, at(i)], src[...], 1, 0)

    fill(1, lb)
    slope(0, la, sa)

    def body(k, _):
        fill(2 * k + 2, la)
        slope(2 * k + 1, lb, sb)
        add(2 * k, sa)
        fill(2 * k + 3, lb)
        slope(2 * k + 2, la, sa)
        add(2 * k + 1, sb)
        return 0

    lax.fori_loop(0, n // 2 - 1, body, 0)
    slope(n - 1, lb, sb)
    add(n - 2, sa)
    add(n - 1, sb)
    for z in range(8):
        q, k = encode(acc[:, z * 256 : (z + 1) * 256])
        out_ref[z, 0:128, :] = q
        out_ref[z, 128:144, :] = jnp.broadcast_to(k, (16, 256))


def centroid_grads(base, es, st, c, T=1024):
    return pl.pallas_call(
        lambda *r: centroid_kernel(T, *r),
        in_specs=[pl.BlockSpec(memory_space=pltpu.SMEM)] + [VM] * 6,
        out_specs=VM,
        out_shape=jax.ShapeDtypeStruct((8, 144, 256), jnp.int16),
        scratch_shapes=[
            pltpu.VMEM((4096, 128), BF16),
            pltpu.VMEM((128, 4096), BF16),
            pltpu.VMEM((4096, 8), F32),
            pltpu.VMEM((128, 2048), F32),
            pltpu.VMEM((T, 2048), F32),
            pltpu.VMEM((T, 2048), F32),
            pltpu.VMEM((T, 2048), BF16),
            pltpu.VMEM((T, 2048), BF16),
        ],
        compiler_params=params(48),
        cost_estimate=cost(12 * 2**30, 2**23),
        name="centroid_grads",
    )(base, *es, st, c)


def total_of(parts):
    total = None
    for ref in parts:
        part = ref[0:128, :].astype(F32) * scale_of(ref[128:144, :])[0:1]
        total = part if total is None else total + part
    return total.T * SCALE


def sum_tokens_kernel(*refs):
    refs[8][...] = total_of(refs[:8])


def sum_tokens(r):
    return pl.pallas_call(
        sum_tokens_kernel,
        in_specs=[VM] * 8,
        out_specs=VM,
        out_shape=jax.ShapeDtypeStruct((128, 128), F32),
        cost_estimate=cost(2**18),
        name="sum_tokens",
    )(*r)


def sum_kernel(in_ref, out_ref):
    q, k = encode(total_of([in_ref.at[z] for z in range(8)]))
    block = jnp.concatenate([q, jnp.broadcast_to(k, (16, 128))], axis=0)
    for z in range(8):
        out_ref[z] = block


def sum_planes(r):
    return pl.pallas_call(
        sum_kernel,
        in_specs=[VM],
        out_specs=VM,
        out_shape=jax.ShapeDtypeStruct((8, 272, 128), jnp.int16),
        cost_estimate=cost(2**22),
        name="sum_planes",
    )(r)


def widen(r):
    return r[:, 0:256, :].astype(F32) * scale_of(r[:, 256:257, :])


def shift(x, axis, k):
    return lax.ppermute(x, axis, [(i, (i + k) % 4) for i in range(4)])


def ring(x, axis):
    return [x] + [shift(x, axis, k) for k in RING[1:]]


def exchange(x, me, steps):
    blocks = [lax.dynamic_index_in_dim(x, me ^ k, 0, keepdims=False) for k in steps]
    return [
        lax.ppermute(b, ("y", "c"), [(i, i ^ k) for i in range(8)]) if k else b
        for b, k in zip(blocks, steps)
    ]


def local(token_embeds, centroids, targets, token_weights):
    info = jnp.stack([token_weights.astype(F32), targets.astype(F32)])
    info = jnp.concatenate([info, jnp.zeros((6, 128), F32)], axis=0)
    x, y, core = lax.axis_index("x"), lax.axis_index("y"), lax.axis_index("c")
    cent = y * 2 + core
    base = jnp.stack([cent * 8192, x * 2048, x, y, core]).astype(jnp.int32)
    pair = jnp.concatenate([token_embeds, lax.ppermute(token_embeds, "c", [(0, 1), (1, 0)])], axis=0)
    group = jnp.concatenate(ring(pair, "y"), axis=0)
    plane = ring(group, "x")
    stats = pass_one(base, group, centroids, info)
    stats, *plane = lax.optimization_barrier((stats, *plane))
    stats = lax.all_to_all(stats, ("x", "y", "c"), 0, 0, tiled=True)
    codes = centroid_grads(base, plane, stats, centroids)
    codes = lax.all_to_all(codes, "z", 0, 0, tiled=True)
    token_codes = token_grads(base, group, stats, centroids)
    early = exchange(token_codes, cent, (0, 1, 4))
    codes, *early = lax.optimization_barrier((codes, *early))
    codes = sum_planes(codes)
    codes, token_codes = lax.optimization_barrier((codes, token_codes))
    parts = early + exchange(token_codes, cent, (2, 3, 5, 6, 7))
    codes = lax.all_to_all(codes, "z", 0, 0, tiled=True)
    codes = lax.all_gather(codes, "x", axis=0, tiled=True)
    return sum_tokens(parts), widen(codes).reshape(8192, 128)


def solution(mesh):
    torus = jax.sharding.Mesh(mesh.devices.reshape(8, 4, 4, 2), ("z", "x", "y", "c"))
    tokens = P(("z", "x", "y", "c"))
    return jax.shard_map(
        local,
        mesh=torus,
        in_specs=(P(("z", "x", "y", "c"), None), P(("y", "c"), None), tokens, tokens),
        out_specs=(P(("z", "x", "y", "c"), None), P(("y", "c"), None)),
        check_vma=False,
    )
```

```python
import math

import jax
import jax.numpy as jnp
from jax import lax
from jax.experimental import pallas as pl
from jax.experimental.pallas import tpu as pltpu
from jax.sharding import PartitionSpec as P

SCALE = 1.0 / math.sqrt(128.0)
RATE = math.log2(math.e) / math.sqrt(128.0)
F32 = jnp.float32
BF16 = jnp.bfloat16
TOP = 32700.0
STEPS = 32.0
VM = pl.BlockSpec(memory_space=pltpu.VMEM)
SM = pl.BlockSpec(memory_space=pltpu.SMEM)
RING = (0, 1, 3, 2)


def dot(a, b, ca, cb):
    return lax.dot_general(a, b, (((ca,), (cb,)), ((), ())), preferred_element_type=F32)


def params(mib):
    return pltpu.CompilerParams(vmem_limit_bytes=mib * 2**20)


def cost(flops, transcendentals=0):
    return pl.CostEstimate(flops=flops, bytes_accessed=2**21, transcendentals=transcendentals)


def encode(x):
    largest = jnp.max(jnp.abs(x), axis=0, keepdims=True)
    k = jnp.ceil(jnp.log2(jnp.maximum(largest, 1e-35)) * STEPS)
    q = jnp.round(x * (jnp.exp2(k * (-1.0 / STEPS)) * TOP))
    return q.astype(jnp.int32).astype(jnp.int16), k.astype(jnp.int32).astype(jnp.int16)


def scale_of(k):
    return jnp.exp2(k.astype(F32) * (1.0 / STEPS)) * (1.0 / TOP)


def pass_one_kernel(rows, e_ref, c_ref, info_ref, out_ref, la, lb):
    T = 1024
    n = c_ref.shape[0] // rows

    def fill(i, dst, m):
        c = c_ref[pl.ds(pl.multiple_of(i * rows, rows), rows), :]
        l = dot(c, e_ref[...], 1, 1)
        dst[...] = l
        return jnp.maximum(m, jnp.max(l.reshape(rows // 8, 8, T), axis=0))

    def add(src, s, m_of_s, m):
        l = src[...].reshape(rows // 8, 8, T)
        return s * jnp.exp2((m_of_s - m) * RATE) + jnp.sum(jnp.exp2((l - m[None]) * RATE), axis=0)

    m_old = jnp.full((8, T), -3.0e38, F32)
    s = jnp.zeros((8, T), F32)
    m = fill(0, la, m_old)

    def body(k, state):
        m_old, m, s = state
        m_b = fill(2 * k + 1, lb, m)
        s = add(la, s, m_old, m)
        m_a = fill(2 * k + 2, la, m_b)
        s = add(lb, s, m, m_b)
        return m_b, m_a, s

    m_old, m, s = lax.fori_loop(0, n // 2 - 1, body, (m_old, m, s))
    m_b = fill(n - 1, lb, m)
    s = add(la, s, m_old, m)
    s = add(lb, s, m, m_b)
    m = m_b
    peak = jnp.max(m, axis=0, keepdims=True)
    total = jnp.sum(s * jnp.exp2((m - peak) * RATE), axis=0, keepdims=True)
    cut = [slice(j * 128, (j + 1) * 128) for j in range(8)]
    stats = jnp.concatenate([peak[:, c] for c in cut] + [total[:, c] for c in cut], axis=0)
    for i in range(32):
        out_ref[i, 0:16, :] = stats
        out_ref[i, 16:24, :] = info_ref[...]


def pass_one(e, c, info, rows=1024):
    return pl.pallas_call(
        lambda *r: pass_one_kernel(rows, *r),
        in_specs=[VM, VM, VM],
        out_specs=VM,
        out_shape=jax.ShapeDtypeStruct((32, 24, 128), F32),
        scratch_shapes=[
            pltpu.VMEM((rows, 1024), F32),
            pltpu.VMEM((rows, 1024), F32),
        ],
        compiler_params=params(24),
        cost_estimate=cost(8 * 2**30, 2**23),
        name="pass_one",
    )(e, c, info)


def combine(x_ref, x):
    parts = [x_ref[x * 8 + i] for i in range(8)]
    m = parts[0][0:8]
    for v in parts[1:]:
        m = jnp.maximum(m, v[0:8])
    s = sum(v[8:16] * jnp.exp2((v[0:8] - m) * RATE) for v in parts)
    w = jnp.concatenate([v[16:17] for v in parts], axis=0)
    g = jnp.concatenate([v[17:18] for v in parts], axis=0)
    return m, w / s, w, g


def token_kernel(rows, base_ref, e_ref, st_ref, c_ref, out_ref, M, R, W, G, acc, la, lb, sa, sb):
    T = 1024
    n = c_ref.shape[0] // rows
    sub = lax.broadcasted_iota(jnp.int32, (8, 128), 0)
    m, r, w, g = combine(st_ref, base_ref[2])
    for j in range(8):
        sl = slice(j * 128, (j + 1) * 128)
        M[:, sl] = jnp.broadcast_to(m[j : j + 1], (8, 128))
        R[:, sl] = jnp.broadcast_to(r[j : j + 1], (8, 128))
        W[:, sl] = jnp.broadcast_to(w[j : j + 1], (8, 128))
        G[:, sl] = jnp.broadcast_to(g[j : j + 1], (8, 128)).astype(jnp.int32) - sub - base_ref[0]
    acc[...] = jnp.zeros_like(acc)

    def at(i):
        return pl.ds(pl.multiple_of(i * rows, rows), rows)

    def fill(i, dst):
        dst[...] = dot(c_ref[at(i), :], e_ref[...], 1, 1)

    def slope(i, src, dst):
        l = src[...].reshape(rows // 8, 8, T)
        p = jnp.exp2((l - M[...][None]) * RATE) * R[...][None]
        k8 = lax.broadcasted_iota(jnp.int32, (rows // 8, 8, T), 0) * 8
        p = p - jnp.where((G[...] - i * rows)[None] == k8, W[...][None], 0.0)
        dst[...] = p.reshape(rows, T).astype(BF16)

    def add(i, src):
        acc[...] += dot(c_ref[at(i), :], src[...], 0, 0)

    fill(0, la)
    fill(1, lb)
    slope(0, la, sa)

    def body(k, _):
        fill(2 * k + 2, la)
        slope(2 * k + 1, lb, sb)
        add(2 * k, sa)
        fill(2 * k + 3, lb)
        slope(2 * k + 2, la, sa)
        add(2 * k + 1, sb)
        return 0

    lax.fori_loop(0, n // 2 - 1, body, 0)
    slope(n - 1, lb, sb)
    add(n - 2, sa)
    add(n - 1, sb)
    for j in range(8):
        q, k = encode(acc[:, j * 128 : (j + 1) * 128])
        out_ref[j, 0:128, :] = q
        out_ref[j, 128:144, :] = jnp.broadcast_to(k, (16, 128))


def token_grads(base, e, st, c, rows=2048):
    return pl.pallas_call(
        lambda *r: token_kernel(rows, *r),
        in_specs=[SM, VM, VM, VM],
        out_specs=VM,
        out_shape=jax.ShapeDtypeStruct((8, 144, 128), jnp.int16),
        scratch_shapes=[
        ]
        + [pltpu.VMEM((8, 1024), F32)] * 3
        + [pltpu.VMEM((8, 1024), jnp.int32), pltpu.VMEM((128, 1024), F32)]
        + [pltpu.VMEM((rows, 1024), F32)] * 2
        + [pltpu.VMEM((rows, 1024), BF16)] * 2,
        compiler_params=params(40),
        cost_estimate=cost(12 * 2**30, 2**23),
        name="token_grads",
    )(base, e, st, c)


def centroid_kernel(T, base_ref, e0, e1, e2, e3, st_ref, c_ref, out_ref, E, ET, ST, acc, la, lb, sa, sb):
    N = 2048
    n = 4096 // T
    c = c_ref[pl.ds(pl.multiple_of(base_ref[1], N), N), :]
    la[...] = dot(e0[...], c, 1, 1)
    for x, e in enumerate((e0, e1, e2, e3)):
        E[x * 1024 : (x + 1) * 1024, :] = e[...]
    for x, step in enumerate((0, 3, 1, 2)):
        stats = combine(st_ref, lax.rem(base_ref[2] + step, 4))
        for j in range(8):
            b = x * 8 + j
            tile = jnp.concatenate([v[j : j + 1] for v in stats] + [jnp.zeros((4, 128), F32)], axis=0)
            ST[b * 128 : (b + 1) * 128, :] = tile.T
        ET[:, x * 1024 : (x + 1) * 1024] = E[x * 1024 : (x + 1) * 1024, :].T
    acc[...] = jnp.zeros_like(acc)
    base = base_ref[0] + base_ref[1]

    def at(i):
        return pl.ds(pl.multiple_of(i * T, T), T)

    def fill(i, dst):
        dst[...] = dot(E[at(i), :], c, 1, 1)

    def slope(i, src, dst):
        st = ST[at(i), :]
        p = jnp.exp2((src[...] - st[:, 0:1]) * RATE) * st[:, 1:2]
        place = lax.broadcasted_iota(jnp.int32, (T, N), 1)
        hit = (st[:, 3:4].astype(jnp.int32) - base) == place
        dst[...] = (p - jnp.where(hit, st[:, 2:3], 0.0)).astype(BF16)

    def add(i, src):
        acc[...] += dot(ET[:, at(i)], src[...], 1, 0)

    fill(1, lb)
    slope(0, la, sa)

    def body(k, _):
        fill(2 * k + 2, la)
        slope(2 * k + 1, lb, sb)
        add(2 * k, sa)
        fill(2 * k + 3, lb)
        slope(2 * k + 2, la, sa)
        add(2 * k + 1, sb)
        return 0

    lax.fori_loop(0, n // 2 - 1, body, 0)
    slope(n - 1, lb, sb)
    add(n - 2, sa)
    add(n - 1, sb)
    for z in range(8):
        q, k = encode(acc[:, z * 256 : (z + 1) * 256])
        out_ref[z, 0:128, :] = q
        out_ref[z, 128:144, :] = jnp.broadcast_to(k, (16, 256))


def centroid_grads(base, es, st, c, T=1024):
    return pl.pallas_call(
        lambda *r: centroid_kernel(T, *r),
        in_specs=[pl.BlockSpec(memory_space=pltpu.SMEM)] + [VM] * 6,
        out_specs=VM,
        out_shape=jax.ShapeDtypeStruct((8, 144, 256), jnp.int16),
        scratch_shapes=[
            pltpu.VMEM((4096, 128), BF16),
            pltpu.VMEM((128, 4096), BF16),
            pltpu.VMEM((4096, 8), F32),
            pltpu.VMEM((128, 2048), F32),
            pltpu.VMEM((T, 2048), F32),
            pltpu.VMEM((T, 2048), F32),
            pltpu.VMEM((T, 2048), BF16),
            pltpu.VMEM((T, 2048), BF16),
        ],
        compiler_params=params(48),
        cost_estimate=cost(12 * 2**30, 2**23),
        name="centroid_grads",
    )(base, *es, st, c)


def total_of(parts):
    total = None
    for ref in parts:
        part = ref[0:128, :].astype(F32) * scale_of(ref[128:144, :])[0:1]
        total = part if total is None else total + part
    return total.T * SCALE


def sum_tokens_kernel(*refs):
    refs[8][...] = total_of(refs[:8])


def sum_tokens(r):
    return pl.pallas_call(
        sum_tokens_kernel,
        in_specs=[VM] * 8,
        out_specs=VM,
        out_shape=jax.ShapeDtypeStruct((128, 128), F32),
        cost_estimate=cost(2**18),
        name="sum_tokens",
    )(*r)


def sum_kernel(in_ref, out_ref):
    q, k = encode(total_of([in_ref.at[z] for z in range(8)]))
    block = jnp.concatenate([q, jnp.broadcast_to(k, (16, 128))], axis=0)
    for z in range(8):
        out_ref[z] = block


def sum_planes(r):
    return pl.pallas_call(
        sum_kernel,
        in_specs=[VM],
        out_specs=VM,
        out_shape=jax.ShapeDtypeStruct((8, 272, 128), jnp.int16),
        cost_estimate=cost(2**22),
        name="sum_planes",
    )(r)


def widen(r):
    return r[:, 0:256, :].astype(F32) * scale_of(r[:, 256:257, :])


def shift(x, axis, k):
    return lax.ppermute(x, axis, [(i, (i + k) % 4) for i in range(4)])


def ring(x, axis):
    return [x] + [shift(x, axis, k) for k in RING[1:]]


def exchange(x, me, steps):
    blocks = [lax.dynamic_index_in_dim(x, me ^ k, 0, keepdims=False) for k in steps]
    return [
        lax.ppermute(b, ("y", "c"), [(i, i ^ k) for i in range(8)]) if k else b
        for b, k in zip(blocks, steps)
    ]


def local(token_embeds, centroids, targets, token_weights):
    info = jnp.stack([token_weights.astype(F32), targets.astype(F32)])
    info = jnp.concatenate([info, jnp.zeros((6, 128), F32)], axis=0)
    x, y, core = lax.axis_index("x"), lax.axis_index("y"), lax.axis_index("c")
    cent = y * 2 + core
    base = jnp.stack([cent * 8192, x * 2048, x, y]).astype(jnp.int32)
    pair = lax.all_gather(token_embeds, "c", axis=0, tiled=True)
    spread = jnp.broadcast_to(pair[None], (4, 256, 128))
    group = lax.all_to_all(spread, "y", 0, 0, tiled=True).reshape(1024, 128)
    plane = ring(group, "x")
    stats = pass_one(group, centroids, info)
    stats, *plane = lax.optimization_barrier((stats, *plane))
    stats = lax.all_to_all(stats, ("x", "y", "c"), 0, 0, tiled=True)
    codes = centroid_grads(base, plane, stats, centroids)
    codes = lax.all_to_all(codes, "z", 0, 0, tiled=True)
    token_codes = token_grads(base, group, stats, centroids)
    early = exchange(token_codes, cent, (0, 1, 4))
    codes, *early = lax.optimization_barrier((codes, *early))
    codes = sum_planes(codes)
    codes, token_codes = lax.optimization_barrier((codes, token_codes))
    parts = early + exchange(token_codes, cent, (2, 3, 5, 6, 7))
    codes = lax.all_to_all(codes, "z", 0, 0, tiled=True)
    codes = lax.all_gather(codes, "x", axis=0, tiled=True)
    return sum_tokens(parts), widen(codes).reshape(8192, 128)


def solution(mesh):
    torus = jax.sharding.Mesh(mesh.devices.reshape(8, 4, 4, 2), ("z", "x", "y", "c"))
    tokens = P(("z", "x", "y", "c"))
    return jax.shard_map(
        local,
        mesh=torus,
        in_specs=(P(("z", "x", "y", "c"), None), P(("y", "c"), None), tokens, tokens),
        out_specs=(P(("z", "x", "y", "c"), None), P(("y", "c"), None)),
        check_vma=False,
    )
```

```python
import math

import jax
import jax.numpy as jnp
from jax import lax
from jax.experimental import pallas as pl
from jax.experimental.pallas import tpu as pltpu
from jax.sharding import PartitionSpec as P

SCALE = 1.0 / math.sqrt(128.0)
RATE = math.log2(math.e) / math.sqrt(128.0)
F32 = jnp.float32
BF16 = jnp.bfloat16
TOP = 32700.0
STEPS = 32.0
VM = pl.BlockSpec(memory_space=pltpu.VMEM)
SM = pl.BlockSpec(memory_space=pltpu.SMEM)
RING = (0, 1, 3, 2)


def dot(a, b, ca, cb):
    return lax.dot_general(a, b, (((ca,), (cb,)), ((), ())), preferred_element_type=F32)


def params(mib):
    return pltpu.CompilerParams(vmem_limit_bytes=mib * 2**20)


def cost(flops, transcendentals=0):
    return pl.CostEstimate(flops=flops, bytes_accessed=2**21, transcendentals=transcendentals)


def encode(x):
    largest = jnp.max(jnp.abs(x), axis=0, keepdims=True)
    k = jnp.ceil(jnp.log2(jnp.maximum(largest, 1e-35)) * STEPS)
    q = jnp.round(x * (jnp.exp2(k * (-1.0 / STEPS)) * TOP))
    return q.astype(jnp.int32).astype(jnp.int16), k.astype(jnp.int32).astype(jnp.int16)


def scale_of(k):
    return jnp.exp2(k.astype(F32) * (1.0 / STEPS)) * (1.0 / TOP)


def pass_one_kernel(rows, e_ref, c_ref, info_ref, out_ref, la, lb):
    T = 1024
    n = c_ref.shape[0] // rows

    def fill(i, dst, m):
        c = c_ref[pl.ds(pl.multiple_of(i * rows, rows), rows), :]
        l = dot(c, e_ref[...], 1, 1)
        dst[...] = l
        return jnp.maximum(m, jnp.max(l.reshape(rows // 8, 8, T), axis=0))

    def add(src, s, m_of_s, m):
        l = src[...].reshape(rows // 8, 8, T)
        return s * jnp.exp2((m_of_s - m) * RATE) + jnp.sum(jnp.exp2((l - m[None]) * RATE), axis=0)

    m_old = jnp.full((8, T), -3.0e38, F32)
    s = jnp.zeros((8, T), F32)
    m = fill(0, la, m_old)

    def body(k, state):
        m_old, m, s = state
        m_b = fill(2 * k + 1, lb, m)
        s = add(la, s, m_old, m)
        m_a = fill(2 * k + 2, la, m_b)
        s = add(lb, s, m, m_b)
        return m_b, m_a, s

    m_old, m, s = lax.fori_loop(0, n // 2 - 1, body, (m_old, m, s))
    m_b = fill(n - 1, lb, m)
    s = add(la, s, m_old, m)
    s = add(lb, s, m, m_b)
    m = m_b
    peak = jnp.max(m, axis=0, keepdims=True)
    total = jnp.sum(s * jnp.exp2((m - peak) * RATE), axis=0, keepdims=True)
    cut = [slice(j * 128, (j + 1) * 128) for j in range(8)]
    stats = jnp.concatenate([peak[:, c] for c in cut] + [total[:, c] for c in cut], axis=0)
    for i in range(32):
        out_ref[i, 0:16, :] = stats
        out_ref[i, 16:24, :] = info_ref[...]


def pass_one(e, c, info, rows=1024):
    return pl.pallas_call(
        lambda *r: pass_one_kernel(rows, *r),
        in_specs=[VM, VM, VM],
        out_specs=VM,
        out_shape=jax.ShapeDtypeStruct((32, 24, 128), F32),
        scratch_shapes=[
            pltpu.VMEM((rows, 1024), F32),
            pltpu.VMEM((rows, 1024), F32),
        ],
        compiler_params=params(24),
        cost_estimate=cost(8 * 2**30, 2**23),
        name="pass_one",
    )(e, c, info)


def combine(x_ref, x):
    parts = [x_ref[x * 8 + i] for i in range(8)]
    m = parts[0][0:8]
    for v in parts[1:]:
        m = jnp.maximum(m, v[0:8])
    s = sum(v[8:16] * jnp.exp2((v[0:8] - m) * RATE) for v in parts)
    w = jnp.concatenate([v[16:17] for v in parts], axis=0)
    g = jnp.concatenate([v[17:18] for v in parts], axis=0)
    return m, w / s, w, g


def token_kernel(rows, base_ref, e_ref, st_ref, c_ref, out_ref, M, R, W, G, acc, la, lb, sa, sb):
    T = 1024
    n = c_ref.shape[0] // rows
    sub = lax.broadcasted_iota(jnp.int32, (8, 128), 0)
    m, r, w, g = combine(st_ref, base_ref[2])
    for j in range(8):
        sl = slice(j * 128, (j + 1) * 128)
        M[:, sl] = jnp.broadcast_to(m[j : j + 1], (8, 128))
        R[:, sl] = jnp.broadcast_to(r[j : j + 1], (8, 128))
        W[:, sl] = jnp.broadcast_to(w[j : j + 1], (8, 128))
        G[:, sl] = jnp.broadcast_to(g[j : j + 1], (8, 128)).astype(jnp.int32) - sub - base_ref[0]
    acc[...] = jnp.zeros_like(acc)

    def at(i):
        return pl.ds(pl.multiple_of(i * rows, rows), rows)

    def fill(i, dst):
        dst[...] = dot(c_ref[at(i), :], e_ref[...], 1, 1)

    def slope(i, src, dst):
        l = src[...].reshape(rows // 8, 8, T)
        p = jnp.exp2((l - M[...][None]) * RATE) * R[...][None]
        k8 = lax.broadcasted_iota(jnp.int32, (rows // 8, 8, T), 0) * 8
        p = p - jnp.where((G[...] - i * rows)[None] == k8, W[...][None], 0.0)
        dst[...] = p.reshape(rows, T).astype(BF16)

    def add(i, src):
        acc[...] += dot(c_ref[at(i), :], src[...], 0, 0)

    fill(0, la)
    fill(1, lb)
    slope(0, la, sa)

    def body(k, _):
        fill(2 * k + 2, la)
        slope(2 * k + 1, lb, sb)
        add(2 * k, sa)
        fill(2 * k + 3, lb)
        slope(2 * k + 2, la, sa)
        add(2 * k + 1, sb)
        return 0

    lax.fori_loop(0, n // 2 - 1, body, 0)
    slope(n - 1, lb, sb)
    add(n - 2, sa)
    add(n - 1, sb)
    for j in range(8):
        q, k = encode(acc[:, j * 128 : (j + 1) * 128])
        out_ref[j, 0:128, :] = q
        out_ref[j, 128:144, :] = jnp.broadcast_to(k, (16, 128))


def token_grads(base, e, st, c, rows=2048):
    return pl.pallas_call(
        lambda *r: token_kernel(rows, *r),
        in_specs=[SM, VM, VM, VM],
        out_specs=VM,
        out_shape=jax.ShapeDtypeStruct((8, 144, 128), jnp.int16),
        scratch_shapes=[
        ]
        + [pltpu.VMEM((8, 1024), F32)] * 3
        + [pltpu.VMEM((8, 1024), jnp.int32), pltpu.VMEM((128, 1024), F32)]
        + [pltpu.VMEM((rows, 1024), F32)] * 2
        + [pltpu.VMEM((rows, 1024), BF16)] * 2,
        compiler_params=params(40),
        cost_estimate=cost(12 * 2**30, 2**23),
        name="token_grads",
    )(base, e, st, c)


def centroid_kernel(T, base_ref, e0, e1, e2, e3, st_ref, c_ref, out_ref, E, ET, ST, acc, la, lb, sa, sb):
    N = 2048
    n = 4096 // T
    c = c_ref[pl.ds(pl.multiple_of(base_ref[1], N), N), :]
    la[...] = dot(e0[...], c, 1, 1)
    for x, e in enumerate((e0, e1, e2, e3)):
        E[x * 1024 : (x + 1) * 1024, :] = e[...]
    for x, step in enumerate((0, 3, 1, 2)):
        stats = combine(st_ref, lax.rem(base_ref[2] + step, 4))
        for j in range(8):
            b = x * 8 + j
            tile = jnp.concatenate([v[j : j + 1] for v in stats] + [jnp.zeros((4, 128), F32)], axis=0)
            ST[b * 128 : (b + 1) * 128, :] = tile.T
        ET[:, x * 1024 : (x + 1) * 1024] = E[x * 1024 : (x + 1) * 1024, :].T
    acc[...] = jnp.zeros_like(acc)
    base = base_ref[0] + base_ref[1]

    def at(i):
        return pl.ds(pl.multiple_of(i * T, T), T)

    def fill(i, dst):
        dst[...] = dot(E[at(i), :], c, 1, 1)

    def slope(i, src, dst):
        st = ST[at(i), :]
        p = jnp.exp2((src[...] - st[:, 0:1]) * RATE) * st[:, 1:2]
        place = lax.broadcasted_iota(jnp.int32, (T, N), 1)
        hit = (st[:, 3:4].astype(jnp.int32) - base) == place
        dst[...] = (p - jnp.where(hit, st[:, 2:3], 0.0)).astype(BF16)

    def add(i, src):
        acc[...] += dot(ET[:, at(i)], src[...], 1, 0)

    fill(1, lb)
    slope(0, la, sa)

    def body(k, _):
        fill(2 * k + 2, la)
        slope(2 * k + 1, lb, sb)
        add(2 * k, sa)
        fill(2 * k + 3, lb)
        slope(2 * k + 2, la, sa)
        add(2 * k + 1, sb)
        return 0

    lax.fori_loop(0, n // 2 - 1, body, 0)
    slope(n - 1, lb, sb)
    add(n - 2, sa)
    add(n - 1, sb)
    for z in range(8):
        q, k = encode(acc[:, z * 256 : (z + 1) * 256])
        out_ref[z, 0:128, :] = q
        out_ref[z, 128:144, :] = jnp.broadcast_to(k, (16, 256))


def centroid_grads(base, es, st, c, T=1024):
    return pl.pallas_call(
        lambda *r: centroid_kernel(T, *r),
        in_specs=[pl.BlockSpec(memory_space=pltpu.SMEM)] + [VM] * 6,
        out_specs=VM,
        out_shape=jax.ShapeDtypeStruct((8, 144, 256), jnp.int16),
        scratch_shapes=[
            pltpu.VMEM((4096, 128), BF16),
            pltpu.VMEM((128, 4096), BF16),
            pltpu.VMEM((4096, 8), F32),
            pltpu.VMEM((128, 2048), F32),
            pltpu.VMEM((T, 2048), F32),
            pltpu.VMEM((T, 2048), F32),
            pltpu.VMEM((T, 2048), BF16),
            pltpu.VMEM((T, 2048), BF16),
        ],
        compiler_params=params(48),
        cost_estimate=cost(12 * 2**30, 2**23),
        name="centroid_grads",
    )(base, *es, st, c)


def total_of(parts):
    total = None
    for ref in parts:
        part = ref[0:128, :].astype(F32) * scale_of(ref[128:144, :])[0:1]
        total = part if total is None else total + part
    return total.T * SCALE


def sum_tokens_kernel(*refs):
    refs[8][...] = total_of(refs[:8])


def sum_tokens(r):
    return pl.pallas_call(
        sum_tokens_kernel,
        in_specs=[VM] * 8,
        out_specs=VM,
        out_shape=jax.ShapeDtypeStruct((128, 128), F32),
        cost_estimate=cost(2**18),
        name="sum_tokens",
    )(*r)


def sum_kernel(in_ref, out_ref):
    q, k = encode(total_of([in_ref.at[z] for z in range(8)]))
    block = jnp.concatenate([q, jnp.broadcast_to(k, (16, 128))], axis=0)
    for z in range(8):
        out_ref[z] = block


def sum_planes(r):
    return pl.pallas_call(
        sum_kernel,
        in_specs=[VM],
        out_specs=VM,
        out_shape=jax.ShapeDtypeStruct((8, 272, 128), jnp.int16),
        cost_estimate=cost(2**22),
        name="sum_planes",
    )(r)


def widen(r):
    return r[:, 0:256, :].astype(F32) * scale_of(r[:, 256:257, :])


def shift(x, axis, k):
    return lax.ppermute(x, axis, [(i, (i + k) % 4) for i in range(4)])


def ring(x, axis):
    return [x] + [shift(x, axis, k) for k in RING[1:]]


def exchange(x, me, steps):
    blocks = [lax.dynamic_index_in_dim(x, me ^ k, 0, keepdims=False) for k in steps]
    return [
        lax.ppermute(b, ("y", "c"), [(i, i ^ k) for i in range(8)]) if k else b
        for b, k in zip(blocks, steps)
    ]


def local(token_embeds, centroids, targets, token_weights):
    info = jnp.stack([token_weights.astype(F32), targets.astype(F32)])
    info = jnp.concatenate([info, jnp.zeros((6, 128), F32)], axis=0)
    x, y, core = lax.axis_index("x"), lax.axis_index("y"), lax.axis_index("c")
    cent = y * 2 + core
    base = jnp.stack([cent * 8192, x * 2048, x, y]).astype(jnp.int32)
    pair = lax.all_gather(token_embeds, "c", axis=0, tiled=True)
    spread = jnp.broadcast_to(pair[None], (4, 256, 128))
    group = lax.all_to_all(spread, "y", 0, 0, tiled=True).reshape(1024, 128)
    plane = ring(group, "x")
    stats = pass_one(group, centroids, info)
    stats, *plane = lax.optimization_barrier((stats, *plane))
    stats = lax.all_to_all(stats, ("x", "y", "c"), 0, 0, tiled=True)
    codes = centroid_grads(base, plane, stats, centroids)
    codes = lax.all_to_all(codes, "z", 0, 0, tiled=True)
    token_codes = token_grads(base, group, stats, centroids)
    early = exchange(token_codes, cent, (0, 1, 2))
    codes, *early = lax.optimization_barrier((codes, *early))
    codes = sum_planes(codes)
    codes, token_codes = lax.optimization_barrier((codes, token_codes))
    parts = early + exchange(token_codes, cent, (3, 4, 5, 6, 7))
    codes = lax.all_to_all(codes, "z", 0, 0, tiled=True)
    codes = lax.all_gather(codes, "x", axis=0, tiled=True)
    return sum_tokens(parts), widen(codes).reshape(8192, 128)


def solution(mesh):
    torus = jax.sharding.Mesh(mesh.devices.reshape(8, 4, 4, 2), ("z", "x", "y", "c"))
    tokens = P(("z", "x", "y", "c"))
    return jax.shard_map(
        local,
        mesh=torus,
        in_specs=(P(("z", "x", "y", "c"), None), P(("y", "c"), None), tokens, tokens),
        out_specs=(P(("z", "x", "y", "c"), None), P(("y", "c"), None)),
        check_vma=False,
    )
```
